32 devices in a mesh: groups: 2 (over x), replica: 8 (over z, y), tensor: 2 (over core).
Axes of the slice: x: 2, y: 2, z: 4, core: 2. Of those that a mesh axis runs over, the one named last changes fastest.
Arguments:
- ssm_state: bfloat16 [256, 128, 64, 128], P(('groups', 'replica'), 'tensor'), parts along dimension 0, may hold values from -6 to 6
- tail_inner: bfloat16 [256, 3, 8192], P(('groups', 'replica'), None, 'tensor'), parts along dimension 0, may hold values from -6 to 6
- tail_groups: bfloat16 [256, 3, 2, 512], P(('groups', 'replica'), None, None, 'tensor'), parts along dimension 0, may hold values from -6 to 6
- key_cache: bfloat16 [256, 4, 256, 128], P(('groups', 'replica'), 'tensor'), parts along dimension 0, may hold values from -6 to 6
- value_cache: bfloat16 [256, 4, 256, 128], P(('groups', 'replica'), 'tensor'), parts along dimension 0, may hold values from -6 to 6
- cache_length: int32 [256], P('groups'), parts along dimension 0, may hold values from 32 to 256, as said below
- finished: int32 [256], P('groups'), parts along dimension 0, may hold values from 0 to 1, as said below
- source: int32 [256], P(('groups', 'replica')), parts along dimension 0, may hold values from 0 to 127, as said below
- new_inner: bfloat16 [256, 4, 8192], P(('groups', 'replica'), None, 'tensor'), parts along dimension 0, may hold values from -6 to 6
- new_gate: bfloat16 [256, 4, 8192], P(('groups', 'replica'), None, 'tensor'), parts along dimension 0, may hold values from -6 to 6
- new_groups: bfloat16 [256, 4, 2, 512], P(('groups', 'replica'), None, None, 'tensor'), parts along dimension 0, may hold values from -6 to 6
- new_delta: bfloat16 [256, 4, 128], P(('groups', 'replica'), None, 'tensor'), parts along dimension 0, may hold values from -4 to 4
- new_query: bfloat16 [256, 4, 4096], P(('groups', 'replica'), None, 'tensor'), parts along dimension 0, may hold values from -8 to 8
- new_entries: bfloat16 [256, 4, 2, 512], P(('groups', 'replica'), None, None, 'tensor'), parts along dimension 0, may hold values from -8 to 8
- filter_inner: float32 [4, 8192], P(None, 'tensor'), may hold values from -3 to 3
- filter_groups: float32 [4, 2, 512], P(None, None, 'tensor'), may hold values from -3 to 3
- decay_rate: float32 [128], P('tensor'), may hold values from 0.02 to 1
- delta_bias: float32 [128], P('tensor'), may hold values from -1.5 to 0.5
- skip_gain: float32 [128], P('tensor'), may hold values from 0.5 to 1.5
- norm_gain: float32 [8192], P('tensor'), may hold values from 0.1 to 1.9
Outputs:
- mixer_output: bfloat16 [256, 4, 8192], P(('groups', 'replica'), None, 'tensor'), parts along dimension 0
- attention_output: bfloat16 [256, 4, 4096], P(('groups', 'replica'), None, 'tensor'), parts along dimension 0
The draws below stay inside these ranges and needn't reach their ends.
There are 2 independent parts, one for each index of `groups`. The reference program is written for one: setup_inputs(seed, part) draws one part's arguments, and reference() takes and returns one part's arrays. A program takes and returns all parts, laid end to end along the dimension named above; an argument that names none is the same for every part. Nothing has to cross between parts.
Inputs may be any that keep to these rules, and one draw needn't show every extreme that they name: source is a permutation of the 128 slots of a group; a rollout that stays on its replica keeps its slot; each replica hands exactly 7 rollouts to other replicas and takes exactly 7 from them, at most one between any two replicas. finished is 0 for every rollout that changes replica. `cache_length`: some entry equals 256 in every draw.
All inputs are finite; a program needn't handle non-finite values.
Results may differ from the reference program's by a relative error of at most 0.0049.
Values may be sent and summed in bfloat16 or wider, within the bound.
A program may use at most 192 MiB of HBM per device.

```python
import math
import jax
import jax.numpy as jnp
from jax import lax

ROLL_DEV = 16
LMAX = 256
STEPS = 4
CONV = 4
HEADS = 128
HEAD_DIM = 64
STATE = 128
GROUPS = 4
QHEADS = 32
KV_HEADS = 4
HEAD = 128
INNER = 8192
MOVE_DEV = 7
ROLLOUTS = 128
N_REPLICA = 8


def migration(key):
    key = jax.random.fold_in(key, 11)
    order_key, slot_key = jax.random.split(key)
    ranking = jax.random.permutation(order_key, N_REPLICA).astype(jnp.int32)
    position = jnp.zeros((N_REPLICA,), jnp.int32).at[ranking].set(jnp.arange(N_REPLICA, dtype=jnp.int32))
    chosen_slots = jax.vmap(lambda item: jax.random.permutation(item, ROLL_DEV))(jax.random.split(slot_key, N_REPLICA))
    chosen_slots = chosen_slots[:, :MOVE_DEV].astype(jnp.int32)
    receiver = jnp.arange(N_REPLICA, dtype=jnp.int32)[:, None]
    offsets = jnp.arange(MOVE_DEV, dtype=jnp.int32)[None, :]
    sender = ranking[(position[receiver] - offsets - 1) % N_REPLICA]
    target = receiver * ROLL_DEV + chosen_slots
    anchor = sender * ROLL_DEV + chosen_slots[sender, offsets]
    source = jnp.arange(ROLLOUTS, dtype=jnp.int32).at[target.reshape(-1)].set(anchor.reshape(-1))
    return source.astype(jnp.int32)


def draw_new_query(key, part):
    key = jax.random.fold_in(key, 7)
    query = 2.0 * jax.random.normal(key, (ROLLOUTS, STEPS, QHEADS * HEAD), jnp.float32)
    return jnp.clip(query, -8.0, 8.0).astype(jnp.bfloat16)


def draw_new_entries(key, part):
    key = jax.random.fold_in(key, 5)
    entries = jax.random.normal(key, (ROLLOUTS, STEPS, 2, KV_HEADS * HEAD), jnp.float32)
    return jnp.clip(entries, -8.0, 8.0).astype(jnp.bfloat16)


def draw_cache_length(key, part):
    key = jax.random.fold_in(key, 3)
    first_key, second_key = jax.random.split(key)
    lengths = jax.random.randint(first_key, (ROLLOUTS,), max(1, LMAX // 8), LMAX + 1)
    longest = jax.random.randint(second_key, (), 0, ROLLOUTS)
    return jnp.where(jnp.arange(ROLLOUTS) == longest, LMAX, lengths).astype(jnp.int32)


def draw_source(key, part):
    return migration(key)


def draw_finished(key, part):
    source = migration(key)
    key = jax.random.fold_in(key, 13)
    marks = (jax.random.randint(key, (ROLLOUTS,), 0, 4) == 0).astype(jnp.int32)
    slots = jnp.arange(ROLLOUTS, dtype=jnp.int32)
    leaving = jnp.zeros((ROLLOUTS,), jnp.int32).at[source].set((source != slots).astype(jnp.int32))
    return jnp.where(leaving == 1, 0, marks).astype(jnp.int32)


def shard_levels(stream_key, extent, shards, least, top_value):
    factor_of, own = 1.0, jax.random.fold_in(stream_key, 6)
    for dim, parts in shards:
        steps = jnp.exp(jax.random.uniform(jax.random.fold_in(own, dim), (parts,), jnp.float32, least / len(shards), top_value / len(shards)))
        factor_of = factor_of * jnp.repeat(steps, extent[dim] // parts).reshape([-1 if axis == dim else 1 for axis in range(len(extent))])
    return factor_of


def normal_values(key, extent, deviation, bound, cuts=(), kind=jnp.bfloat16):
    values = deviation * jax.random.normal(key, extent, jnp.float32)
    if cuts:
        values = values * shard_levels(key, extent, cuts, -0.22, 0.18)
    return jnp.clip(values, -bound, bound).astype(kind)


def setup_inputs(seed: int = 0, part: int = 0) -> dict:
    streams_of = jax.random.split(jax.random.key(seed), 21)
    part_keys = jax.random.split(jax.random.fold_in(streams_of[20], part), 21)
    ssm_state = normal_values(part_keys[0], (ROLLOUTS, HEADS, HEAD_DIM, STATE), 1.0, 6.0, ((0, 8), (1, 2)))
    tail_inner = normal_values(part_keys[1], (ROLLOUTS, CONV - 1, INNER), 1.0, 6.0, ((0, 8), (2, 2)))
    tail_groups = normal_values(part_keys[2], (ROLLOUTS, CONV - 1, 2, GROUPS * STATE), 1.0, 6.0, ((0, 8), (3, 2)))
    key_cache = normal_values(part_keys[3], (ROLLOUTS, KV_HEADS, LMAX, HEAD), 1.0, 6.0, ((0, 8), (1, 2)))
    value_cache = normal_values(part_keys[4], (ROLLOUTS, KV_HEADS, LMAX, HEAD), 1.0, 6.0, ((0, 8), (1, 2)))
    cache_length = draw_cache_length(jax.random.fold_in(jax.random.fold_in(streams_of[20], part), 71), part)
    finished = draw_finished(jax.random.fold_in(jax.random.fold_in(streams_of[20], part), 71), part)
    source = draw_source(jax.random.fold_in(jax.random.fold_in(streams_of[20], part), 71), part)
    new_inner = normal_values(part_keys[8], (ROLLOUTS, STEPS, INNER), 1.0, 6.0, ((0, 8), (2, 2)))
    new_gate = normal_values(part_keys[9], (ROLLOUTS, STEPS, INNER), 1.0, 6.0, ((0, 8), (2, 2)))
    new_groups = normal_values(part_keys[10], (ROLLOUTS, STEPS, 2, GROUPS * STATE), 1.0, 6.0, ((0, 8), (3, 2)))
    new_delta = normal_values(part_keys[11], (ROLLOUTS, STEPS, HEADS), 1.0, 4.0, ((0, 8), (2, 2)))
    new_query = draw_new_query(jax.random.fold_in(jax.random.fold_in(streams_of[20], part), 71), part)
    new_entries = draw_new_entries(jax.random.fold_in(jax.random.fold_in(streams_of[20], part), 71), part)
    filter_inner = normal_values(streams_of[14], (CONV, INNER), CONV ** -0.5, 3.0, ((1, 2),), jnp.float32)
    filter_groups = normal_values(streams_of[15], (CONV, 2, GROUPS * STATE), CONV ** -0.5, 3.0, ((2, 2),), jnp.float32)
    decay_rate = jnp.clip(jnp.exp(math.log(1.0) - 3.912023 * jax.random.uniform(streams_of[16], (HEADS,), jnp.float32) ** shard_levels(streams_of[16], (HEADS,), ((0, 2),), -0.2, 0.2)), 0.02, 1.0)
    delta_bias = jnp.clip(-1.5 + 2.0 * jax.random.uniform(streams_of[17], (HEADS,), jnp.float32) ** shard_levels(streams_of[17], (HEADS,), ((0, 2),), -0.2, 0.2), -1.5, 0.5)
    skip_gain = jnp.clip(0.5 + 1.0 * jax.random.uniform(streams_of[18], (HEADS,), jnp.float32) ** shard_levels(streams_of[18], (HEADS,), ((0, 2),), -0.2, 0.2), 0.5, 1.5)
    norm_gain = jnp.clip(1.0 + 0.18 * jax.random.normal(streams_of[19], (INNER,), jnp.float32), 0.1, 1.9)
    return {"ssm_state": ssm_state, "tail_inner": tail_inner, "tail_groups": tail_groups, "key_cache": key_cache, "value_cache": value_cache, "cache_length": cache_length, "finished": finished, "source": source, "new_inner": new_inner, "new_gate": new_gate, "new_groups": new_groups, "new_delta": new_delta, "new_query": new_query, "new_entries": new_entries, "filter_inner": filter_inner, "filter_groups": filter_groups, "decay_rate": decay_rate, "delta_bias": delta_bias, "skip_gain": skip_gain, "norm_gain": norm_gain}


def filtered(history, recent, weights):
    window = jnp.concatenate([history, recent], axis=1).astype(jnp.float32)
    length = recent.shape[1]
    summed = weights[0] * window[:, 0:length]
    for offset in range(1, weights.shape[0]):
        summed = summed + weights[offset] * window[:, offset:offset + length]
    return jax.nn.silu(summed)

def mixer(ssm_prior, history_inner, history_groups, new_inner, new_gate, new_groups, new_delta, filter_inner, filter_groups, decay_rate, delta_bias, skip_gain, norm_gain):
    batch_size, step_count, inner_width = new_inner.shape
    head_count, head_size, state_width = (ssm_prior.shape[1], ssm_prior.shape[2], ssm_prior.shape[3])
    group_count = new_groups.shape[3] // state_width
    inputs = filtered(history_inner, new_inner, filter_inner).reshape(batch_size, step_count, head_count, head_size)
    mixing = filtered(history_groups, new_groups, filter_groups).reshape(batch_size, step_count, 2, group_count, 1, state_width)
    mixing = jnp.broadcast_to(mixing, (batch_size, step_count, 2, group_count, head_count // group_count, state_width))
    mixing = mixing.reshape(batch_size, step_count, 2, head_count, state_width)
    timestep = jax.nn.softplus(new_delta.astype(jnp.float32) + delta_bias)
    retention = jnp.exp(-decay_rate * timestep)
    carried = ssm_prior.astype(jnp.float32)
    results = []
    for position in range(step_count):
        injected = (timestep[:, position, :, None] * inputs[:, position])[..., None] * mixing[:, position, 0, :, None, :]
        carried = retention[:, position, :, None, None] * carried + injected
        readout = jnp.einsum('bhpn,bhn->bhp', carried, mixing[:, position, 1], precision=lax.Precision.HIGHEST)
        results.append(readout + skip_gain[:, None] * inputs[:, position])
    combined = jnp.stack(results, axis=1).reshape(batch_size, step_count, inner_width)
    gated_rows = combined * jax.nn.silu(new_gate.astype(jnp.float32))
    grouped = gated_rows.reshape(batch_size, step_count, group_count, inner_width // group_count)
    inverse_rms = lax.rsqrt(lax.optimization_barrier(jnp.mean(grouped * grouped, axis=-1, keepdims=True)) + 1e-05)
    return (grouped * inverse_rms).reshape(batch_size, step_count, inner_width) * norm_gain

def attention(queries, recent, key_cache, value_cache, lengths):
    batch_size, step_count = (queries.shape[0], queries.shape[1])
    shared_heads, cache_span, head_size = (key_cache.shape[1], key_cache.shape[2], key_cache.shape[3])
    grouped = queries.reshape(batch_size, step_count, shared_heads, -1, head_size).astype(jnp.float32)
    entries = recent.reshape(batch_size, step_count, 2, shared_heads, head_size).astype(jnp.float32)
    factor = 1.0 / math.sqrt(head_size)
    cached_scores = jnp.einsum('bsjgd,bjld->bjsgl', grouped, key_cache.astype(jnp.float32), preferred_element_type=jnp.float32) * factor
    recent_scores = jnp.einsum('bsjgd,btjd->bjsgt', grouped, entries[:, :, 0], preferred_element_type=jnp.float32) * factor
    visible = jnp.arange(cache_span)[None, :] < lengths[:, None]
    cached_scores = jnp.where(visible[:, None, None, None, :], cached_scores, -jnp.inf)
    causal = jnp.arange(step_count)[None, :] <= jnp.arange(step_count)[:, None]
    recent_scores = jnp.where(causal[None, None, :, None, :], recent_scores, -jnp.inf)
    highest = jnp.maximum(lax.optimization_barrier(jnp.max(cached_scores, axis=-1)), lax.optimization_barrier(jnp.max(recent_scores, axis=-1)))[..., None]
    cached_weight = jnp.exp(cached_scores - highest)
    recent_weight = jnp.exp(recent_scores - highest)
    denominator = lax.optimization_barrier(jnp.sum(cached_weight, axis=-1, keepdims=True)) + lax.optimization_barrier(jnp.sum(recent_weight, axis=-1, keepdims=True))
    cached_prob = (cached_weight / denominator).astype(jnp.bfloat16).astype(jnp.float32)
    recent_prob = (recent_weight / denominator).astype(jnp.bfloat16).astype(jnp.float32)
    attended = jnp.einsum('bjsgl,bjld->bsjgd', cached_prob, value_cache.astype(jnp.float32), preferred_element_type=jnp.float32)
    attended = attended + jnp.einsum('bjsgt,btjd->bsjgd', recent_prob, entries[:, :, 1], preferred_element_type=jnp.float32)
    return attended.reshape(batch_size, step_count, -1)

def reference(ssm_state, tail_inner, tail_groups, key_cache, value_cache, cache_length, finished, source, new_inner, new_gate, new_groups, new_delta, new_query, new_entries, filter_inner, filter_groups, decay_rate, delta_bias, skip_gain, norm_gain):

    def block(index):
        start = (index * ROLL_DEV).astype(jnp.int32)
        chosen = lax.dynamic_slice_in_dim(source, start, ROLL_DEV).astype(jnp.int32)

        def local(array):
            return lax.dynamic_slice_in_dim(array, start, ROLL_DEV)

        def moved(array):
            return jnp.take(array, chosen, axis=0)
        keeping = (1 - moved(finished)).astype(jnp.float32)[:, None, None]
        combined = mixer(moved(ssm_state), moved(tail_inner), moved(tail_groups), local(new_inner), local(new_gate), local(new_groups), local(new_delta), filter_inner, filter_groups, decay_rate, delta_bias, skip_gain, norm_gain)
        attended = attention(local(new_query), local(new_entries), moved(key_cache), moved(value_cache), moved(cache_length))
        return ((combined * keeping).astype(jnp.bfloat16), (attended * keeping).astype(jnp.bfloat16))
    mixer_blocks, attention_blocks = lax.map(block, jnp.arange(N_REPLICA, dtype=jnp.int32))
    return (mixer_blocks.reshape(ROLLOUTS, STEPS, INNER), attention_blocks.reshape(ROLLOUTS, STEPS, QHEADS * HEAD))
```

```python
import functools
import math

import jax
import jax.numpy as jnp
from jax import lax
from jax.experimental import pallas as pl
from jax.experimental.pallas import tpu as pltpu
from jax.sharding import PartitionSpec as P

F32 = jnp.float32
BF16 = jnp.bfloat16
MESH = pl.DeviceIdType.MESH
VMEM_BYTES = 48 * 1024 * 1024


def greet(n, me):
    barrier = pltpu.get_barrier_semaphore()
    for d in range(1, n):
        peer = lax.rem(me + d, n)
        pl.semaphore_signal(barrier, inc=1, device_id={"replica": peer}, device_id_type=MESH)
    pl.semaphore_wait(barrier, n - 1)


def forward_kernel(n, rows, pick_ref, packed_ref, list_ref, out_ref, lists_ref, staged, sems, send_sem, recv_sem, lsend_sem, lrecv_sem):
    me = lax.axis_index("replica")
    keep = pltpu.make_async_copy(packed_ref, out_ref.at[pl.ds(0, rows)], sems.at[0])
    keep.start()
    own = pltpu.make_async_copy(list_ref, lists_ref.at[me], sems.at[1])
    own.start()
    greet(n, me)
    copies = []
    for d in range(1, n):
        peer = lax.rem(me + d, n)
        staged[d] = packed_ref[pick_ref[peer]]
        for src, dst, ss, rs in (
            (list_ref, lists_ref.at[me], lsend_sem, lrecv_sem),
            (staged.at[d], out_ref.at[rows + me], send_sem, recv_sem),
        ):
            copy = pltpu.make_async_remote_copy(
                src_ref=src,
                dst_ref=dst,
                send_sem=ss.at[d],
                recv_sem=rs.at[d],
                device_id={"replica": peer},
                device_id_type=MESH,
            )
            copy.start()
            copies.append(copy)
    keep.wait()
    own.wait()
    for copy in copies:
        copy.wait()


def back_kernel(n, rows, wide, pick_ref, done_ref, mixer_ref, attn_ref, held, sems, send_sem, recv_sem):
    me = lax.axis_index("replica")
    greet(n, me)
    copies = []
    for d in range(1, n):
        peer = lax.rem(me + d, n)
        copy = pltpu.make_async_remote_copy(
            src_ref=done_ref.at[rows + peer],
            dst_ref=held.at[rows + me],
            send_sem=send_sem.at[d],
            recv_sem=recv_sem.at[d],
            device_id={"replica": peer},
            device_id_type=MESH,
        )
        copy.start()
        copies.append(copy)
    keep = pltpu.make_async_copy(done_ref.at[pl.ds(0, rows)], held.at[pl.ds(0, rows)], sems.at[0])
    keep.start()
    keep.wait()
    for copy in copies:
        copy.wait()
    for i in range(rows):
        row = held[pick_ref[i]]
        mixer_ref[i] = row[:, :wide]
        attn_ref[i] = row[:, wide:]


def silu(v):
    return v / (1.0 + jnp.exp(-v))


def split(v):
    high = v.astype(BF16).astype(F32)
    return high, v - high


def step_kernel(
    dims,
    from_ref, to_ref, length_ref, done_ref,
    new_ref, state_ref, ti_ref, tg_ref, key_ref, value_ref,
    fi_ref, fg_ref, rate_ref, bias_ref, skip_ref, gain_ref,
    out_ref,
    expand, wi, wg, mix, cmat, prod, coef, qs, kn, vn,
):
    T, inner, heads, p, n, groups, kv, qh, hd, offs = dims
    j = pl.program_id(0)
    half = groups * n
    @pl.when(j == 0)
    def _():
        row = lax.broadcasted_iota(jnp.int32, (heads, inner), 0)
        col = lax.broadcasted_iota(jnp.int32, (heads, inner), 1)
        expand[...] = jnp.where(col // p == row, 1.0, 0.0).astype(BF16)
        kn[...] = jnp.zeros_like(kn)
        vn[...] = jnp.zeros_like(vn)

    o_inner, o_gate, o_groups, o_delta, o_query, o_entries = offs
    K = fi_ref.shape[0]
    wg[0 : K - 1, 0:half] = tg_ref[0, :, 0, :].astype(F32)
    wg[0 : K - 1, half : 2 * half] = tg_ref[0, :, 1, :].astype(F32)
    wg[K - 1 : K - 1 + T, :] = new_ref[0, :, o_groups : o_groups + 2 * half].astype(F32)
    accB = fg_ref[0, 0:1, :] * wg[0:T, 0:half]
    accC = fg_ref[0, 1:2, :] * wg[0:T, half : 2 * half]
    for k in range(1, K):
        accB = accB + fg_ref[k, 0:1, :] * wg[k : k + T, 0:half]
        accC = accC + fg_ref[k, 1:2, :] * wg[k : k + T, half : 2 * half]
    B = silu(accB)
    C = silu(accC)
    c_high, c_low = split(C)
    cmat[0:T, :] = c_high
    cmat[T : 2 * T, :] = c_low
    cm = cmat[...].astype(BF16)
    per = inner // groups
    reads = []
    for g in range(groups):
        prior = state_ref[0, g * (heads // groups) : (g + 1) * (heads // groups)].reshape(per, n)
        r = lax.dot_general(cm[:, g * n : (g + 1) * n], prior, (((1,), (1,)), ((), ())), preferred_element_type=F32)
        reads.append(r[0:T] + r[T : 2 * T])
    v = new_ref[0, :, o_delta : o_delta + heads].astype(F32) + bias_ref[...]
    ts = jnp.maximum(v, 0.0) + jnp.log1p(jnp.exp(-jnp.abs(v)))
    a = -rate_ref[...] * ts
    tri = lax.broadcasted_iota(jnp.int32, (T, heads), 0)
    cum = jnp.zeros((T, heads), F32)
    for s in range(T):
        cum = cum + jnp.where(tri >= s, a[s : s + 1], 0.0)
    for s in range(T):
        prod[s * 8 : s * 8 + T, :] = C * B[s : s + 1]
    mrow = lax.broadcasted_iota(jnp.int32, (half, heads), 0) // n
    mcol = lax.broadcasted_iota(jnp.int32, (half, heads), 1) // (heads // groups)
    gmap = jnp.where(mrow == mcol, 1.0, 0.0)
    cb = jnp.dot(prod[...], gmap, preferred_element_type=F32, precision=lax.Precision.HIGHEST)
    for s in range(T + 1):
        if s < T:
            decay = jnp.exp(jnp.where(tri >= s, cum - cum[s : s + 1], -1e30))
            block = cb[s * 8 : s * 8 + T] * decay * ts[s : s + 1]
            block = block + jnp.where(tri == s, skip_ref[...], 0.0)
        else:
            block = jnp.exp(cum)
        high, low = split(block)
        coef[s * 8 : s * 8 + T, :] = high
        coef[s * 8 + T : s * 8 + 2 * T, :] = low
    cf = coef[...].astype(BF16)
    keep = (1 - done_ref[j]).astype(F32)
    for g in range(groups):
        lanes = slice(g * per, (g + 1) * per)
        wide = jnp.dot(cf, expand[:, lanes], preferred_element_type=F32)
        wi[0 : K - 1, :] = ti_ref[0, :, lanes].astype(F32)
        wi[K - 1 : K - 1 + T, :] = new_ref[0, :, o_inner + g * per : o_inner + (g + 1) * per].astype(F32)
        acc = fi_ref[0:1, lanes] * wi[0:T, :]
        for k in range(1, K):
            acc = acc + fi_ref[k : k + 1, lanes] * wi[k : k + T, :]
        x = silu(acc)
        y = reads[g] * (wide[T * 8 : T * 8 + T] + wide[T * 8 + T : T * 8 + 2 * T])
        for s in range(T):
            y = y + (wide[s * 8 : s * 8 + T] + wide[s * 8 + T : s * 8 + 2 * T]) * x[s : s + 1]
        gate = new_ref[0, :, o_gate + g * per : o_gate + (g + 1) * per].astype(F32)
        y = y * silu(gate)
        inv = lax.rsqrt(jnp.mean(y * y, axis=-1, keepdims=True) + 1e-05)
        out_ref[0, :, lanes] = (y * inv * gain_ref[:, lanes] * keep).astype(BF16)
    length = length_ref[j]
    span = key_ref.shape[2]
    R = qh * T
    factor = 1.0 / math.sqrt(hd)
    pos = lax.broadcasted_iota(jnp.int32, (R, span), 1)
    rr = lax.broadcasted_iota(jnp.int32, (R, 16), 0) % T
    rc = lax.broadcasted_iota(jnp.int32, (R, 16), 1)
    for h in range(kv):
        for q in range(qh):
            at = o_query + (h * qh + q) * hd
            qs[h, q * T : (q + 1) * T, :] = new_ref[0, :, at : at + hd].astype(F32)
        at = o_entries + h * hd
        kn[h, 0:T, :] = new_ref[0, :, at : at + hd].astype(F32)
        at = o_entries + (kv + h) * hd
        vn[h, 0:T, :] = new_ref[0, :, at : at + hd].astype(F32)
        query = qs[h].astype(BF16)
        nt = (((1,), (1,)), ((), ()))
        old = lax.dot_general(query, key_ref[0, h], nt, preferred_element_type=F32) * factor
        new = lax.dot_general(query, kn[h].astype(BF16), nt, preferred_element_type=F32) * factor
        old = jnp.where(pos < length, old, -1e30)
        new = jnp.where(rc <= rr, new, -1e30)
        top = jnp.maximum(jnp.max(old, axis=-1, keepdims=True), jnp.max(new, axis=-1, keepdims=True))
        old = jnp.exp(old - top)
        new = jnp.exp(new - top)
        total = jnp.sum(old, axis=-1, keepdims=True) + jnp.sum(new, axis=-1, keepdims=True)
        old = (old / total).astype(BF16)
        new = (new / total).astype(BF16)
        got = jnp.dot(old, value_ref[0, h], preferred_element_type=F32)
        got = got + jnp.dot(new, vn[h].astype(BF16), preferred_element_type=F32)
        got = got * keep
        for q in range(qh):
            at = inner + (h * qh + q) * hd
            out_ref[0, :, at : at + hd] = got[q * T : (q + 1) * T].astype(BF16)


def body(
    ssm_state, tail_inner, tail_groups, key_cache, value_cache, cache_length, finished, source,
    new_inner, new_gate, new_groups, new_delta, new_query, new_entries,
    filter_inner, filter_groups, decay_rate, delta_bias, skip_gain, norm_gain,
):
    n = lax.axis_size("replica")
    me = lax.axis_index("replica")
    rows, heads, p, width = ssm_state.shape
    T, inner = new_inner.shape[1:]
    kv, span, hd = key_cache.shape[1:]
    groups = new_groups.shape[3] // width
    qwide = new_query.shape[2]
    qh = qwide // (kv * hd)
    pieces = [
        new_inner,
        new_gate,
        new_groups.reshape(rows, T, -1),
        jnp.pad(new_delta, ((0, 0), (0, 0), (0, -heads % 128))),
        new_query,
        new_entries.reshape(rows, T, -1),
    ]
    offs, total = [], 0
    for piece in pieces:
        offs.append(total)
        total += piece.shape[2]
    packed = jnp.concatenate(pieces, axis=2)
    home = source // rows
    slots = jnp.arange(rows, dtype=jnp.int32)
    peers = jnp.arange(n, dtype=jnp.int32)
    ask = jnp.sum(jnp.where(home[None, :] == peers[:, None], slots[None, :], 0), axis=1)
    ask = jnp.where(peers == me, 0, ask)
    listed = jnp.broadcast_to(jnp.pad(source, (0, 128 - rows))[None, :], (8, 128))

    hbm = pl.BlockSpec(memory_space=pl.ANY)
    vmem = pl.BlockSpec(memory_space=pltpu.VMEM)
    smem = pl.BlockSpec(memory_space=pltpu.SMEM)
    dma = pltpu.SemaphoreType.DMA
    inputs, lists = pl.pallas_call(
        functools.partial(forward_kernel, n, rows),
        out_shape=(
            jax.ShapeDtypeStruct((rows + n, T, total), BF16),
            jax.ShapeDtypeStruct((n, 8, 128), jnp.int32),
        ),
        in_specs=[smem, vmem, vmem],
        out_specs=(hbm, hbm),
        scratch_shapes=[
            pltpu.VMEM((n, T, total), BF16),
            dma((2,)), dma((n,)), dma((n,)), dma((n,)), dma((n,)),
        ],
        compiler_params=pltpu.CompilerParams(collective_id=0, has_side_effects=True, vmem_limit_bytes=VMEM_BYTES),
    )(ask, packed, listed)

    everywhere = lists[:, 0, :rows]
    mine = (me * rows + slots)[:, None, None] == everywhere[None, :, :]
    taker = jnp.sum(jnp.where(mine, peers[None, :, None], 0), axis=(1, 2))
    place = jnp.where(taker == me, slots, rows + taker).astype(jnp.int32)
    lengths = lax.dynamic_slice_in_dim(cache_length, me * rows, rows)
    done = lax.dynamic_slice_in_dim(finished, me * rows, rows)

    dims = (T, inner, heads, p, width, groups, kv, qh, hd, tuple(offs))
    owide = inner + qwide

    def at(shape):
        zeros = (0,) * (len(shape) - 1)
        return pl.BlockSpec((1,) + shape[1:], lambda j, *_: (j,) + zeros)

    def whole(a):
        zeros = (0,) * a.ndim
        return pl.BlockSpec(a.shape, lambda j, *_: zeros)

    params = [filter_inner, filter_groups, decay_rate[None], delta_bias[None], skip_gain[None], norm_gain[None]]
    half = groups * width
    outs = pl.pallas_call(
        functools.partial(step_kernel, dims),
        out_shape=jax.ShapeDtypeStruct((rows + n, T, owide), BF16),
        grid_spec=pltpu.PrefetchScalarGridSpec(
            num_scalar_prefetch=4,
            grid=(rows,),
            in_specs=[
                pl.BlockSpec((1, T, total), lambda j, f, *_: (f[j], 0, 0)),
                at(ssm_state.shape), at(tail_inner.shape), at(tail_groups.shape),
                at(key_cache.shape), at(value_cache.shape),
            ] + [whole(a) for a in params],
            out_specs=pl.BlockSpec((1, T, owide), lambda j, f, t, *_: (t[j], 0, 0)),
            scratch_shapes=[
                pltpu.VMEM((heads, inner), BF16),
                pltpu.VMEM((8, inner // groups), F32),
                pltpu.VMEM((8, 2 * half), F32),
                pltpu.VMEM((8, 2 * half), F32),
                pltpu.VMEM((2 * T, half), F32),
                pltpu.VMEM((T * 8, half), F32),
                pltpu.VMEM((T * 8 + 8, heads), F32),
                pltpu.VMEM((kv, qh * T, hd), F32),
                pltpu.VMEM((kv, 16, hd), F32),
                pltpu.VMEM((kv, 16, hd), F32),
            ],
        ),
        compiler_params=pltpu.CompilerParams(vmem_limit_bytes=VMEM_BYTES),
    )(place, place, lengths, done, inputs, ssm_state, tail_inner, tail_groups, key_cache, value_cache, *params)

    pick = jnp.where(home == me, slots, rows + home).astype(jnp.int32)
    return pl.pallas_call(
        functools.partial(back_kernel, n, rows, inner),
        out_shape=(
            jax.ShapeDtypeStruct((rows, T, inner), BF16),
            jax.ShapeDtypeStruct((rows, T, qwide), BF16),
        ),
        in_specs=[smem, hbm],
        out_specs=(vmem, vmem),
        scratch_shapes=[
            pltpu.VMEM((rows + n, T, owide), BF16),
            dma((1,)), dma((n,)), dma((n,)),
        ],
        compiler_params=pltpu.CompilerParams(collective_id=1, has_side_effects=True, vmem_limit_bytes=VMEM_BYTES),
    )(pick, outs)


def solution(mesh):
    in_specs = (
        P(("groups", "replica"), "tensor", None, None),
        P(("groups", "replica"), None, "tensor"),
        P(("groups", "replica"), None, None, "tensor"),
        P(("groups", "replica"), "tensor", None, None),
        P(("groups", "replica"), "tensor", None, None),
        P("groups"),
        P("groups"),
        P(("groups", "replica")),
        P(("groups", "replica"), None, "tensor"),
        P(("groups", "replica"), None, "tensor"),
        P(("groups", "replica"), None, None, "tensor"),
        P(("groups", "replica"), None, "tensor"),
        P(("groups", "replica"), None, "tensor"),
        P(("groups", "replica"), None, None, "tensor"),
        P(None, "tensor"),
        P(None, None, "tensor"),
        P("tensor"),
        P("tensor"),
        P("tensor"),
        P("tensor"),
    )
    out_specs = (P(("groups", "replica"), None, "tensor"), P(("groups", "replica"), None, "tensor"))
    return jax.shard_map(body, mesh=mesh, in_specs=in_specs, out_specs=out_specs, check_vma=False)
```

```python
import functools
import math

import jax
import jax.numpy as jnp
from jax import lax
from jax.experimental import pallas as pl
from jax.experimental.pallas import tpu as pltpu
from jax.sharding import PartitionSpec as P

F32 = jnp.float32
BF16 = jnp.bfloat16
MESH = pl.DeviceIdType.MESH
VMEM_BYTES = 60 * 1024 * 1024
TOGETHER = 2


def greet(n, me):
    barrier = pltpu.get_barrier_semaphore()
    for d in range(1, n):
        peer = lax.rem(me + d, n)
        pl.semaphore_signal(barrier, inc=1, device_id={"replica": peer}, device_id_type=MESH)
    pl.semaphore_wait(barrier, n - 1)


def forward_kernel(n, rows, pick_ref, packed_ref, list_ref, out_ref, lists_ref, staged, sems, send_sem, recv_sem, lsend_sem, lrecv_sem):
    me = lax.axis_index("replica")
    keep = pltpu.make_async_copy(packed_ref, out_ref.at[pl.ds(0, rows)], sems.at[0])
    keep.start()
    own = pltpu.make_async_copy(list_ref, lists_ref.at[me], sems.at[1])
    own.start()
    greet(n, me)
    copies = []
    for d in range(1, n):
        peer = lax.rem(me + d, n)
        staged[d] = packed_ref[pick_ref[peer]]
        for src, dst, ss, rs in (
            (list_ref, lists_ref.at[me], lsend_sem, lrecv_sem),
            (staged.at[d], out_ref.at[rows + me], send_sem, recv_sem),
        ):
            copy = pltpu.make_async_remote_copy(
                src_ref=src,
                dst_ref=dst,
                send_sem=ss.at[d],
                recv_sem=rs.at[d],
                device_id={"replica": peer},
                device_id_type=MESH,
            )
            copy.start()
            copies.append(copy)
    keep.wait()
    own.wait()
    for copy in copies:
        copy.wait()


def back_kernel(n, rows, wide, pick_ref, give_ref, done_ref, mixer_ref, attn_ref, held, staged, send_sem, recv_sem):
    me = lax.axis_index("replica")
    greet(n, me)
    copies = []
    for d in range(1, n):
        peer = lax.rem(me + d, n)
        staged[d] = done_ref[give_ref[peer]]
        copy = pltpu.make_async_remote_copy(
            src_ref=staged.at[d],
            dst_ref=held.at[rows + me],
            send_sem=send_sem.at[d],
            recv_sem=recv_sem.at[d],
            device_id={"replica": peer},
            device_id_type=MESH,
        )
        copy.start()
        copies.append(copy)
    for i in range(rows):
        held[i] = done_ref[i]
    for copy in copies:
        copy.wait()
    for i in range(rows):
        row = held[pick_ref[i]]
        mixer_ref[i] = row[:, :wide]
        attn_ref[i] = row[:, wide:]


def silu(v):
    return v / (1.0 + jnp.exp(-v))


def split(v):
    high = v.astype(BF16).astype(F32)
    return high, v - high


def step_kernel(dims, rows, index_ref, *refs):
    T, inner, heads, p, n, groups, kv, qh, hd, offs = dims
    news, refs = refs[:TOGETHER], refs[TOGETHER:]
    slabs, params, out_ref, expand, own = refs[:5], refs[5:11], refs[11], refs[12], refs[13:]

    @pl.when(pl.program_id(0) == 0)
    def _():
        row = lax.broadcasted_iota(jnp.int32, (heads, inner), 0)
        col = lax.broadcasted_iota(jnp.int32, (heads, inner), 1)
        expand[...] = jnp.where(col // p == row, 1.0, 0.0).astype(BF16)
        own[-1][...] = jnp.zeros_like(own[-1])
        own[-2][...] = jnp.zeros_like(own[-2])

    count = (index_ref.shape[0] - rows - 1) // 2
    me = index_ref[index_ref.shape[0] - 1]
    for u in range(TOGETHER):
        slot = me * rows + pl.program_id(0) * TOGETHER + u
        part = [ref.at[pl.ds(u, 1)] for ref in slabs]
        one_slot(
            dims, index_ref[rows + slot], index_ref[rows + count + slot], news[u], *part, *params,
            out_ref.at[pl.ds(u, 1)], expand, *[ref.at[u] for ref in own],
        )


def one_slot(
    dims, length, finished_here,
    new_ref, state_ref, ti_ref, tg_ref, key_ref, value_ref,
    fi_ref, fg_ref, rate_ref, bias_ref, skip_ref, gain_ref,
    out_ref,
    expand, wi, wg, cmat, prod, coef, qs, kn, vn,
):
    T, inner, heads, p, n, groups, kv, qh, hd, offs = dims
    half = groups * n
    o_inner, o_gate, o_groups, o_delta, o_query, o_entries = offs
    K = fi_ref.shape[0]
    wg[0 : K - 1, 0:half] = tg_ref[0, :, 0, :].astype(F32)
    wg[0 : K - 1, half : 2 * half] = tg_ref[0, :, 1, :].astype(F32)
    wg[K - 1 : K - 1 + T, :] = new_ref[0, :, o_groups : o_groups + 2 * half].astype(F32)
    accB = fg_ref[0, 0:1, :] * wg[0:T, 0:half]
    accC = fg_ref[0, 1:2, :] * wg[0:T, half : 2 * half]
    for k in range(1, K):
        accB = accB + fg_ref[k, 0:1, :] * wg[k : k + T, 0:half]
        accC = accC + fg_ref[k, 1:2, :] * wg[k : k + T, half : 2 * half]
    B = silu(accB)
    C = silu(accC)
    c_high, c_low = split(C)
    cmat[0:T, :] = c_high
    cmat[T : 2 * T, :] = c_low
    cm = cmat[...].astype(BF16)
    per = inner // groups
    reads = []
    for g in range(groups):
        prior = state_ref[0, g * (heads // groups) : (g + 1) * (heads // groups)].reshape(per, n)
        r = lax.dot_general(cm[:, g * n : (g + 1) * n], prior, (((1,), (1,)), ((), ())), preferred_element_type=F32)
        reads.append(r[0:T] + r[T : 2 * T])
    v = new_ref[0, :, o_delta : o_delta + heads].astype(F32) + bias_ref[...]
    ts = jnp.maximum(v, 0.0) + jnp.log1p(jnp.exp(-jnp.abs(v)))
    a = -rate_ref[...] * ts
    tri = lax.broadcasted_iota(jnp.int32, (T, heads), 0)
    cum = jnp.zeros((T, heads), F32)
    for s in range(T):
        cum = cum + jnp.where(tri >= s, a[s : s + 1], 0.0)
    for s in range(T):
        prod[s * 8 : s * 8 + T, :] = C * B[s : s + 1]
    mrow = lax.broadcasted_iota(jnp.int32, (half, heads), 0) // n
    mcol = lax.broadcasted_iota(jnp.int32, (half, heads), 1) // (heads // groups)
    gmap = jnp.where(mrow == mcol, 1.0, 0.0)
    cb = jnp.dot(prod[...], gmap, preferred_element_type=F32, precision=lax.Precision.HIGHEST)
    for s in range(T + 1):
        if s < T:
            decay = jnp.exp(jnp.where(tri >= s, cum - cum[s : s + 1], -1e30))
            block = cb[s * 8 : s * 8 + T] * decay * ts[s : s + 1]
            block = block + jnp.where(tri == s, skip_ref[...], 0.0)
        else:
            block = jnp.exp(cum)
        high, low = split(block)
        coef[s * 8 : s * 8 + T, :] = high
        coef[s * 8 + T : s * 8 + 2 * T, :] = low
    cf = coef[...].astype(BF16)
    keep = (1 - finished_here).astype(F32)
    for g in range(groups):
        lanes = slice(g * per, (g + 1) * per)
        wide = jnp.dot(cf, expand[:, lanes], preferred_element_type=F32)
        wi[0 : K - 1, :] = ti_ref[0, :, lanes].astype(F32)
        wi[K - 1 : K - 1 + T, :] = new_ref[0, :, o_inner + g * per : o_inner + (g + 1) * per].astype(F32)
        acc = fi_ref[0:1, lanes] * wi[0:T, :]
        for k in range(1, K):
            acc = acc + fi_ref[k : k + 1, lanes] * wi[k : k + T, :]
        x = silu(acc)
        y = reads[g] * (wide[T * 8 : T * 8 + T] + wide[T * 8 + T : T * 8 + 2 * T])
        for s in range(T):
            y = y + (wide[s * 8 : s * 8 + T] + wide[s * 8 + T : s * 8 + 2 * T]) * x[s : s + 1]
        gate = new_ref[0, :, o_gate + g * per : o_gate + (g + 1) * per].astype(F32)
        y = y * silu(gate)
        inv = lax.rsqrt(jnp.mean(y * y, axis=-1, keepdims=True) + 1e-05)
        out_ref[0, :, lanes] = (y * inv * gain_ref[:, lanes] * keep).astype(BF16)
    span = key_ref.shape[2]
    R = qh * T
    factor = 1.0 / math.sqrt(hd)
    pos = lax.broadcasted_iota(jnp.int32, (R, span), 1)
    rr = lax.broadcasted_iota(jnp.int32, (R, 16), 0) % T
    rc = lax.broadcasted_iota(jnp.int32, (R, 16), 1)
    for h in range(kv):
        for q in range(qh):
            at = o_query + (h * qh + q) * hd
            qs[h, q * T : (q + 1) * T, :] = new_ref[0, :, at : at + hd].astype(F32)
        at = o_entries + h * hd
        kn[h, 0:T, :] = new_ref[0, :, at : at + hd].astype(F32)
        at = o_entries + (kv + h) * hd
        vn[h, 0:T, :] = new_ref[0, :, at : at + hd].astype(F32)
        query = qs[h].astype(BF16)
        nt = (((1,), (1,)), ((), ()))
        old = lax.dot_general(query, key_ref[0, h], nt, preferred_element_type=F32) * factor
        new = lax.dot_general(query, kn[h].astype(BF16), nt, preferred_element_type=F32) * factor
        old = jnp.where(pos < length, old, -1e30)
        new = jnp.where(rc <= rr, new, -1e30)
        top = jnp.maximum(jnp.max(old, axis=-1, keepdims=True), jnp.max(new, axis=-1, keepdims=True))
        old = jnp.exp(old - top)
        new = jnp.exp(new - top)
        total = jnp.sum(old, axis=-1, keepdims=True) + jnp.sum(new, axis=-1, keepdims=True)
        old = (old / total).astype(BF16)
        new = (new / total).astype(BF16)
        got = jnp.dot(old, value_ref[0, h], preferred_element_type=F32)
        got = got + jnp.dot(new, vn[h].astype(BF16), preferred_element_type=F32)
        got = got * keep
        for q in range(qh):
            at = inner + (h * qh + q) * hd
            out_ref[0, :, at : at + hd] = got[q * T : (q + 1) * T].astype(BF16)


def body(
    ssm_state, tail_inner, tail_groups, key_cache, value_cache, cache_length, finished, source,
    new_inner, new_gate, new_groups, new_delta, new_query, new_entries,
    filter_inner, filter_groups, decay_rate, delta_bias, skip_gain, norm_gain,
):
    n = lax.axis_size("replica")
    me = lax.axis_index("replica")
    rows, heads, p, width = ssm_state.shape
    T, inner = new_inner.shape[1:]
    kv, span, hd = key_cache.shape[1:]
    groups = new_groups.shape[3] // width
    qwide = new_query.shape[2]
    qh = qwide // (kv * hd)
    pieces = [
        new_inner,
        new_gate,
        new_groups.reshape(rows, T, -1),
        jnp.pad(new_delta, ((0, 0), (0, 0), (0, -heads % 128))),
        new_query,
        new_entries.reshape(rows, T, -1),
    ]
    offs, total = [], 0
    for piece in pieces:
        offs.append(total)
        total += piece.shape[2]
    packed = jnp.concatenate(pieces, axis=2)
    home = source // rows
    slots = jnp.arange(rows, dtype=jnp.int32)
    peers = jnp.arange(n, dtype=jnp.int32)
    ask = jnp.sum(jnp.where(home[None, :] == peers[:, None], slots[None, :], 0), axis=1)
    ask = jnp.where(peers == me, 0, ask)
    listed = jnp.broadcast_to(jnp.pad(source, (0, 128 - rows))[None, :], (8, 128))

    hbm = pl.BlockSpec(memory_space=pl.ANY)
    vmem = pl.BlockSpec(memory_space=pltpu.VMEM)
    smem = pl.BlockSpec(memory_space=pltpu.SMEM)
    dma = pltpu.SemaphoreType.DMA
    inputs, lists = pl.pallas_call(
        functools.partial(forward_kernel, n, rows),
        out_shape=(
            jax.ShapeDtypeStruct((rows + n, T, total), BF16),
            jax.ShapeDtypeStruct((n, 8, 128), jnp.int32),
        ),
        in_specs=[smem, vmem, vmem],
        out_specs=(hbm, hbm),
        scratch_shapes=[
            pltpu.VMEM((n, T, total), BF16),
            dma((2,)), dma((n,)), dma((n,)), dma((n,)), dma((n,)),
        ],
        compiler_params=pltpu.CompilerParams(collective_id=0, has_side_effects=True, vmem_limit_bytes=VMEM_BYTES),
    )(ask, packed, listed)

    everywhere = lists[:, 0, :rows]
    mine = (me * rows + slots)[:, None, None] == everywhere[None, :, :]
    taker = jnp.sum(jnp.where(mine, peers[None, :, None], 0), axis=(1, 2))
    place = jnp.where(taker == me, slots, rows + taker).astype(jnp.int32)
    index = jnp.concatenate([place, cache_length, finished, me.astype(jnp.int32)[None]])
    give = jnp.sum(jnp.where(mine, slots[:, None, None], 0), axis=(0, 2)).astype(jnp.int32)
    give = jnp.where(peers == me, 0, give)

    dims = (T, inner, heads, p, width, groups, kv, qh, hd, tuple(offs))
    owide = inner + qwide

    def at(shape):
        zeros = (0,) * (len(shape) - 1)
        return pl.BlockSpec((TOGETHER,) + shape[1:], lambda j, *_: (j,) + zeros)

    def whole(a):
        zeros = (0,) * a.ndim
        return pl.BlockSpec(a.shape, lambda j, *_: zeros)

    params = [filter_inner, filter_groups, decay_rate[None], delta_bias[None], skip_gain[None], norm_gain[None]]
    half = groups * width
    outs = pl.pallas_call(
        functools.partial(step_kernel, dims, rows),
        out_shape=jax.ShapeDtypeStruct((rows, T, owide), BF16),
        grid_spec=pltpu.PrefetchScalarGridSpec(
            num_scalar_prefetch=1,
            grid=(rows // TOGETHER,),
            in_specs=[
                pl.BlockSpec((1, T, total), functools.partial(lambda u, j, f: (f[j * TOGETHER + u], 0, 0), u))
                for u in range(TOGETHER)
            ] + [
                at(ssm_state.shape), at(tail_inner.shape), at(tail_groups.shape),
                at(key_cache.shape), at(value_cache.shape),
            ] + [whole(a) for a in params],
            out_specs=at((rows, T, owide)),
            scratch_shapes=[
                pltpu.VMEM((heads, inner), BF16),
                pltpu.VMEM((TOGETHER, 8, inner // groups), F32),
                pltpu.VMEM((TOGETHER, 8, 2 * half), F32),
                pltpu.VMEM((TOGETHER, 2 * T, half), F32),
                pltpu.VMEM((TOGETHER, T * 8, half), F32),
                pltpu.VMEM((TOGETHER, T * 8 + 8, heads), F32),
                pltpu.VMEM((TOGETHER, kv, qh * T, hd), F32),
                pltpu.VMEM((TOGETHER, kv, 16, hd), F32),
                pltpu.VMEM((TOGETHER, kv, 16, hd), F32),
            ],
        ),
        compiler_params=pltpu.CompilerParams(vmem_limit_bytes=VMEM_BYTES),
    )(index, *[inputs] * TOGETHER, ssm_state, tail_inner, tail_groups, key_cache, value_cache, *params)

    pick = jnp.where(home == me, slots, rows + home).astype(jnp.int32)
    return pl.pallas_call(
        functools.partial(back_kernel, n, rows, inner),
        out_shape=(
            jax.ShapeDtypeStruct((rows, T, inner), BF16),
            jax.ShapeDtypeStruct((rows, T, qwide), BF16),
        ),
        in_specs=[smem, smem, vmem],
        out_specs=(vmem, vmem),
        scratch_shapes=[
            pltpu.VMEM((rows + n, T, owide), BF16),
            pltpu.VMEM((n, T, owide), BF16),
            dma((n,)), dma((n,)),
        ],
        compiler_params=pltpu.CompilerParams(collective_id=1, has_side_effects=True, vmem_limit_bytes=VMEM_BYTES),
    )(pick, give, outs)


def solution(mesh):
    in_specs = (
        P(("groups", "replica"), "tensor", None, None),
        P(("groups", "replica"), None, "tensor"),
        P(("groups", "replica"), None, None, "tensor"),
        P(("groups", "replica"), "tensor", None, None),
        P(("groups", "replica"), "tensor", None, None),
        P("groups"),
        P("groups"),
        P(("groups", "replica")),
        P(("groups", "replica"), None, "tensor"),
        P(("groups", "replica"), None, "tensor"),
        P(("groups", "replica"), None, None, "tensor"),
        P(("groups", "replica"), None, "tensor"),
        P(("groups", "replica"), None, "tensor"),
        P(("groups", "replica"), None, None, "tensor"),
        P(None, "tensor"),
        P(None, None, "tensor"),
        P("tensor"),
        P("tensor"),
        P("tensor"),
        P("tensor"),
    )
    out_specs = (P(("groups", "replica"), None, "tensor"), P(("groups", "replica"), None, "tensor"))
    return jax.shard_map(body, mesh=mesh, in_specs=in_specs, out_specs=out_specs, check_vma=False)
```
